128 devices in a mesh: depth: 4 (over y), tile: 32 (over z, x, core).
Axes of the slice: x: 4, y: 4, z: 4, core: 2. Of those that a mesh axis runs over, the one named last changes fastest.
Arguments:
- specimen: float32 [2, 4, 8192, 4096], P(None, 'depth', 'tile'), may hold values from -0.35 to 1.1
- positions: int32 [2, 128], P(None, 'tile'), may hold values from 0 to 7936, as said below
- occupied: int32 [128], P('tile'), may hold values from 0 to 1, as said below
- measured: float32 [128, 256, 256], P('tile'), may hold values from 0.2 to 2
- probe_wave: float32 [2, 256, 256], replicated, may hold values from -4 to 4
Outputs:
- gradient: float32 [2, 4, 8192, 4096], P(None, 'depth', 'tile')
The draws below stay inside these ranges and needn't reach their ends.
Inputs may be any that keep to these rules, and one draw needn't show every extreme that they name: `positions`: column p holds the top row and left column of patch p; the row lies from (p // 4) * 256 to that plus 256 - 1 and never past 8192 - 256; the column lies from 0 to 3840. `occupied`: each aligned block of 4 slots holds 1 to 4 ones, first in the block, then zeros; some block is all ones.
All inputs are finite; a program needn't handle non-finite values.
Results may differ from the reference program's by a relative error of at most 0.0003.
Values sent between devices are 32-bit elements; how exact they have to be, the bound alone decides.
A program may use at most 192 MiB of HBM per device.

```python
import math
import jax
import jax.numpy as jnp
from jax import lax

PATCH = 256
ROWS_DEV = 256
COLS = 4096
SLOTS = 4
SLICES = 4
NROWS = 8192
TOTAL_SLOTS = 128


def draw_specimen(key, part):
    key = jax.random.fold_in(key, 11)
    key_real, key_imag = jax.random.split(key)
    grid_shape = (SLICES, NROWS, COLS)
    real_part = jax.random.uniform(key_real, grid_shape, jnp.float32, 0.7, 1.1)
    imag_part = jax.random.uniform(key_imag, grid_shape, jnp.float32, -0.35, 0.35)
    return jnp.stack([real_part, imag_part]).astype(jnp.float32)


def draw_positions(key, part):
    key = jax.random.fold_in(key, 23)
    key_rows, key_cols = jax.random.split(key)
    slot_ids = jnp.arange(TOTAL_SLOTS, dtype=jnp.int32)
    offsets = jax.random.randint(key_rows, (TOTAL_SLOTS,), 0, ROWS_DEV, dtype=jnp.int32)
    rows_top = jnp.minimum(slot_ids // SLOTS * ROWS_DEV + offsets, NROWS - PATCH)
    columns = jax.random.randint(key_cols, (TOTAL_SLOTS,), 0, COLS - PATCH + 1, dtype=jnp.int32)
    columns = jnp.where(slot_ids == 0, COLS - PATCH, columns)
    return jnp.stack([rows_top, columns]).astype(jnp.int32)


def draw_occupied(key, part):
    key = jax.random.fold_in(key, 37)
    key_count, key_full = jax.random.split(key)
    blocks = TOTAL_SLOTS // SLOTS
    counts = jax.random.randint(key_count, (blocks,), 1, SLOTS + 1, dtype=jnp.int32)
    fullest = jax.random.randint(key_full, (), 0, blocks, dtype=jnp.int32)
    counts = jnp.where(jnp.arange(blocks, dtype=jnp.int32) == fullest, SLOTS, counts)
    slot_ids = jnp.arange(TOTAL_SLOTS, dtype=jnp.int32)
    return (slot_ids % SLOTS < counts[slot_ids // SLOTS]).astype(jnp.int32)


def level_of(stream_key, dims, cuts, least, largest):
    level = 1.0
    for position, parts in cuts:
        heights = jax.random.uniform(jax.random.fold_in(jax.random.fold_in(stream_key, 6), position), (parts,), jnp.float32, least / len(cuts), largest / len(cuts))
        level = level * jnp.repeat(jnp.exp(heights), dims[position] // parts).reshape((-1,) + (1,) * (len(dims) - 1 - position))
    return level


def normal_values(stream_key, dims, width, bound, held_as=jnp.bfloat16):
    return jnp.clip(width * jax.random.normal(stream_key, dims, jnp.float32), -bound, bound).astype(held_as)


def setup_inputs(seed: int = 0) -> dict:
    seeds = jax.random.split(jax.random.key(seed), 6)
    specimen = draw_specimen(jax.random.fold_in(seeds[5], 71), 0)
    positions = draw_positions(jax.random.fold_in(seeds[5], 71), 0)
    occupied = draw_occupied(jax.random.fold_in(seeds[5], 71), 0)
    measured = jnp.clip(jnp.exp(math.log(2.0) - 2.3025851 * jax.random.uniform(seeds[3], (TOTAL_SLOTS, PATCH, PATCH), jnp.float32) ** level_of(seeds[3], (TOTAL_SLOTS, PATCH, PATCH), ((0, 32),), -0.2, 0.2)), 0.2, 2.0)
    probe_wave = normal_values(seeds[4], (2, PATCH, PATCH), 0.7, 4.0, jnp.float32)
    return dict(specimen=specimen, positions=positions, occupied=occupied, measured=measured, probe_wave=probe_wave)


PRECISE = lax.Precision.HIGHEST

def indices(*values):
    return tuple((jnp.asarray(value).astype(jnp.int32) for value in values))

def product(left_side, right_side):
    return jnp.matmul(left_side, right_side, precision=PRECISE)

def complex_times(first_pair, second_pair):
    return (first_pair[0] * second_pair[0] - first_pair[1] * second_pair[1], first_pair[0] * second_pair[1] + first_pair[1] * second_pair[0])

def conjugate(pair):
    return (pair[0], -pair[1])

def transposed(pair):
    return (pair[0].T, pair[1].T)

def complex_left(matrix, values):
    return (product(matrix[0], values[0]) - product(matrix[1], values[1]), product(matrix[0], values[1]) + product(matrix[1], values[0]))

def complex_right(values, matrix):
    return (product(values[0], matrix[0]) - product(values[1], matrix[1]), product(values[0], matrix[1]) + product(values[1], matrix[0]))

def sandwich(left_table, values, right_table):
    return complex_right(complex_left(left_table, values), right_table)

def transform_tables(length):
    counter = jnp.arange(length, dtype=jnp.int32)
    phase_grid = 2.0 * math.pi / length * (counter[:, None] * counter[None, :] % length).astype(jnp.float32)
    norm_factor = 1.0 / math.sqrt(length)
    unitary = (jnp.cos(phase_grid) * norm_factor, -jnp.sin(phase_grid) * norm_factor)
    centred = ((counter + length // 2) % length - length // 2).astype(jnp.float32)
    fresnel = -12.0 * centred * centred / (length * length)
    filter_re = jnp.cos(fresnel)[:, None]
    filter_im = jnp.sin(fresnel)[:, None]
    filtered = (filter_re * unitary[0] - filter_im * unitary[1], filter_re * unitary[1] + filter_im * unitary[0])
    kernel = complex_left(conjugate(unitary), filtered)
    return (unitary, kernel)

def propagate(values, kernel):
    return sandwich(kernel, values, transposed(kernel))

def propagate_back(values, kernel):
    return sandwich(transposed(conjugate(kernel)), values, conjugate(kernel))

def far_residual(values, unitary, target):
    far_field = sandwich(unitary, values, transposed(unitary))
    excess = far_field[0] * far_field[0] + far_field[1] * far_field[1] - target
    scaled = (excess * far_field[0], excess * far_field[1])
    return sandwich(transposed(conjugate(unitary)), scaled, conjugate(unitary))

def reference(specimen, positions, occupied, measured, probe_wave):
    patch_size = probe_wave.shape[-1]
    layers = specimen.shape[1]
    unitary, kernel = transform_tables(patch_size)

    def one_patch(gradient, inputs):
        top_row, left_col, weight, target = inputs
        starts = indices(0, 0, top_row, left_col)
        window = lax.dynamic_slice(specimen, starts, (2, layers, patch_size, patch_size))
        stored = []
        current = (probe_wave[0], probe_wave[1])
        transmitted = current
        for slice_index in range(layers):
            stored.append(current)
            transmitted = complex_times((window[0, slice_index], window[1, slice_index]), current)
            if slice_index < layers - 1:
                current = propagate(transmitted, kernel)
        adjoint = far_residual(transmitted, unitary, target)
        pieces = [None] * layers
        for slice_index in reversed(range(layers)):
            contribution = complex_times(conjugate(stored[slice_index]), adjoint)
            pieces[slice_index] = jnp.stack([contribution[0], contribution[1]]) * weight
            if slice_index > 0:
                reflected = complex_times(conjugate((window[0, slice_index], window[1, slice_index])), adjoint)
                adjoint = propagate_back(reflected, kernel)
        update = jnp.stack(pieces, axis=1)
        existing = lax.dynamic_slice(gradient, starts, update.shape)
        gradient = lax.dynamic_update_slice(gradient, existing + update, starts)
        return (gradient, None)
    weights = occupied.astype(jnp.float32)
    gradient = jnp.zeros(specimen.shape, jnp.float32)
    gradient = lax.scan(one_patch, gradient, (positions[0].astype(jnp.int32), positions[1].astype(jnp.int32), weights, measured))[0]
    return gradient
```

```python
import functools
import math

import jax
import jax.numpy as jnp
import ml_dtypes
import numpy as np
from jax import lax
from jax.experimental import pallas as pl
from jax.experimental.pallas import tpu as pltpu
from jax.sharding import PartitionSpec as P

MESH = pl.DeviceIdType.MESH
BF = jnp.bfloat16
F32 = jnp.float32
N = 256
H = 128
PIECE = (2, N, N)


def transform_tables():
    j = np.arange(N)
    unitary = np.exp(-2j * np.pi * ((j[:, None] * j[None, :]) % N) / N) / math.sqrt(N)
    f = ((j + H) % N) - H
    kernel = np.conj(unitary) @ (np.exp(-12j * f * f / (N * N))[:, None] * unitary)
    kernels = [(kernel[:H, :H] + sign * kernel[:H, H:]) / 2 for sign in (1, -1)]
    halves = [unitary[:H, 0::2], unitary[:H, 1::2]]

    def left(m):
        return np.block([[m.real, -m.imag], [m.imag, m.real]])

    def right(m):
        return np.block([[m.real, m.imag], [-m.imag, m.real]])

    lefts = [[left(m) for m in kernels], [left(m.T) for m in halves], [left(m) for m in halves]]
    rights = [[right(m) for m in kernels], [right(m) for m in halves], [right(m.T) for m in halves]]
    exact = np.array([lefts, rights])
    high = exact.astype(ml_dtypes.bfloat16)
    low = (exact - high.astype(np.float64)).astype(ml_dtypes.bfloat16)
    return np.stack([high, low], axis=3)


def order_table():
    table = np.zeros((N, N))
    table[np.arange(N), np.r_[0:N:2, 1:N:2]] = 1
    return table.astype(ml_dtypes.bfloat16)


def split(x):
    high = x.astype(BF)
    return high, (x - high.astype(F32)).astype(BF)


def dot(a, b):
    return jnp.dot(a, b, preferred_element_type=F32)


def exact_dot(multiply, x):
    high = x.astype(BF)
    rest = x - high.astype(F32)
    middle = rest.astype(BF)
    low = (rest - middle.astype(F32)).astype(BF)
    return multiply(high) + (multiply(middle) + multiply(low))


def put(buf, index, rows, cols, x):
    high, low = split(x)
    buf[index, 0, rows, cols] = high
    buf[index, 1, rows, cols] = low


def half(i):
    return slice(i * H, (i + 1) * H)


def butterfly_store(xr, xi, dbuf):
    for c, x in ((0, xr), (1, xi)):
        top, bottom = x[:H], x[H:]
        for a, y in ((0, top + bottom), (1, top - bottom)):
            put(dbuf, a, half(c), half(0), y[:, :H] + y[:, H:])
            put(dbuf, a, half(c), half(1), y[:, :H] - y[:, H:])


def left_product(kind, tab, dbuf, ebuf):
    for a in range(2):
        high, low = dbuf[a, 0], dbuf[a, 1]
        e = dot(tab[0, kind, a, 0], high) + (dot(tab[0, kind, a, 0], low) + dot(tab[0, kind, a, 1], high))
        for c in range(2):
            for b in range(2):
                put(ebuf, b, half(a), half(c), e[half(c), half(b)])


def right_product(kind, tab, ebuf):
    out = []
    for b in range(2):
        high, low = ebuf[b, 0], ebuf[b, 1]
        out.append(dot(high, tab[1, kind, b, 0]) + (dot(low, tab[1, kind, b, 0]) + dot(high, tab[1, kind, b, 1])))
    return out


def unbutterfly(g):
    res = []
    for c in range(2):
        p, m = g[0][:, half(c)], g[1][:, half(c)]
        y = jnp.concatenate([p + m, p - m], axis=1)
        res.append(jnp.concatenate([y[:H] + y[H:], y[:H] - y[H:]], axis=0))
    return res


def cut(spec, row, col, top, store):
    block = lax.div(col, H)
    rem = lax.rem(col, H)
    odd = lax.rem(block, 2)
    chunk = 32

    def body(i, _):
        rows = pl.ds(pl.multiple_of(i * chunk, chunk), chunk)
        lane = lax.broadcasted_iota(jnp.int32, (chunk, H), 1)
        line = lax.broadcasted_iota(jnp.int32, (chunk, H), 0) + i * chunk
        keep = line >= row if top else line < row
        for side in range(2):
            first = block + (odd if side == 0 else 1 - odd)
            second = first + 2 - 2 * lax.div(first + 2, 32)
            limit = rem * (1 - odd if side == 0 else odd)
            for c in range(2):
                here = spec[first, c, rows, :]
                there = spec[second, c, rows, :]
                store(c, rows, half(side), jnp.where(keep, jnp.where(lane >= limit, here, there), 0.0))
        return 0

    lax.fori_loop(0, N // chunk, body, 0)


def gradient_pieces(
    depth, tiles, specimen, positions, occupied, measured, probe, tables, order,
    own_out, spill_out, before_out,
    spec, mine, halo_out, halo_in, merged, waves, psi, g, dbuf, ebuf, grads, grads_in, tab, perm, meas, mp, wave0,
    pos1, pos2, occ2,
    load_sem, spec_sem, info_send, info_recv, halo_send, halo_recv, far_send, far_recv, y_send, y_recv,
    g_send, g_recv, spill_send, spill_recv, back_send, back_recv, meas_send, meas_recv, out_sem,
):
    d = lax.axis_index("depth")
    t = lax.axis_index("tile")
    odd = lax.rem(t, 2)

    def tile(k):
        return lax.rem(t + k + tiles, tiles)

    def level(k):
        return lax.rem(d + k, depth)

    def remote(src, dst, send, recv, to):
        return pltpu.make_async_remote_copy(
            src_ref=src, dst_ref=dst, send_sem=send, recv_sem=recv, device_id=to, device_id_type=MESH
        )

    far_slot = (odd == 1) & (d >= 2)

    loads = [
        pltpu.make_async_copy(probe, wave0, load_sem.at[0]),
        pltpu.make_async_copy(order, perm, load_sem.at[1]),
        pltpu.make_async_copy(tables, tab, load_sem.at[2]),
    ]
    meas_load = pltpu.make_async_copy(measured.at[d], meas, load_sem.at[3])
    for copy in loads[:2]:
        copy.start()

    @pl.when(jnp.logical_not(far_slot))
    def _():
        meas_load.start()

    def block_load(b):
        cols = pl.ds(pl.multiple_of(b * H, H), H)
        return pltpu.make_async_copy(specimen.at[:, 0, :, cols], spec.at[b], spec_sem.at[b])

    blocks = spec.shape[0]
    lax.fori_loop(0, blocks, lambda b, _: (block_load(b).start(), 0)[1], 0)
    loads[2].start()

    barrier = pltpu.get_barrier_semaphore()
    partners = [(level(k), t) for k in range(1, 4)] + [(d, tile(k)) for k in (-2, -1, 1, 2)]
    for partner in partners:
        pl.semaphore_signal(barrier, inc=1, device_id=partner, device_id_type=MESH)
    pl.semaphore_wait(barrier, len(partners))

    infos = [
        remote(positions, pos1, info_send.at[0], info_recv.at[0], (d, tile(1))),
        remote(positions, pos2, info_send.at[1], info_recv.at[1], (d, tile(2))),
        remote(occupied, occ2, info_send.at[2], info_recv.at[2], (d, tile(2))),
    ]
    for copy in infos:
        copy.start()
    meas_far = remote(measured.at[d], meas, meas_send, meas_recv, (d, tile(2)))
    for copy in infos:
        copy.wait_recv()

    own_row, own_col = positions[0, d], positions[1, d]
    row = jnp.where(far_slot, pos2[0, d], own_row)
    col = jnp.where(far_slot, pos2[1, d], own_col)
    weight = jnp.where(far_slot, occ2[d], occupied[d]).astype(F32)
    loads[0].wait()
    line = lax.broadcasted_iota(jnp.int32, (N, N), 0)
    lane = lax.broadcasted_iota(jnp.int32, (N, N), 1)
    turn_rows = (lax.bitwise_and(line - lane - row, N - 1) == 0).astype(F32).astype(BF)
    turn_cols = (lax.bitwise_and(lane - line - col, N - 1) == 0).astype(F32).astype(BF)
    for c in range(2):
        turned = exact_dot(lambda x: dot(turn_rows, x), wave0[c])
        psi[0, c] = exact_dot(lambda x: dot(x, turn_cols), turned)

    lax.fori_loop(0, blocks, lambda b, _: (block_load(b).wait(), 0)[1], 0)

    def cut_top(k):
        def store(c, rows, cols, x):
            mine[k, c, rows, cols] = x

        cut(spec, positions[0, k] - t * N, positions[1, k], True, store)

    def far_copy(k):
        return remote(mine.at[k], mine.at[k + 2], far_send.at[k - 2], far_recv.at[k - 2], (d, tile(2)))

    def halo_copy(k):
        to = jnp.where((odd == 1) | (k < 2), tile(-1), tile(1))
        return remote(halo_out.at[k], halo_in.at[k], halo_send.at[k], halo_recv.at[k], (d, to))

    @pl.when(odd == 1)
    def _():
        def body(k, _):
            cut_top(k)
            far_copy(k).start()
            return 0

        lax.fori_loop(2, 4, body, 0)

    @pl.when(far_slot)
    def _():
        meas_far.start()

    def cut_bottom(k, _):
        def store(c, rows, cols, x):
            halo_out[k, c, rows, cols] = x

        cut(spec, pos1[0, k] - tile(-1) * N, pos1[1, k], False, store)
        halo_copy(k).start()
        return 0

    lax.fori_loop(0, 4, cut_bottom, 0)

    def cut_mine(k, _):
        cut_top(k)
        return 0

    lax.fori_loop(0, jnp.where(odd == 1, 2, 4), cut_mine, 0)

    def y_copy(k):
        return remote(merged.at[k], waves.at[d], y_send.at[k], y_recv.at[d], (k, t))

    def merge(k, dst):
        halo_copy(k).wait_recv()

        @pl.when((odd == 1) & (k >= 2))
        def _():
            far_copy(k).wait_recv()

        source = jnp.where((odd == 1) & (k >= 2), k + 2, k)

        def body(i, _):
            rows = pl.ds(pl.multiple_of(i * 32, 32), 32)
            for c in range(2):
                dst[c, rows, :] = mine[source, c, rows, :] + halo_in[k, c, rows, :]
            return 0

        lax.fori_loop(0, N // 32, body, 0)

    for j in (1, 3, 2):
        k = level(j)
        merge(k, merged.at[k])
        y_copy(k).start()
    merge(d, waves.at[d])

    def arrived(s):
        @pl.when(s != d)
        def _():
            remote(merged.at[0], waves.at[s], y_send.at[0], y_recv.at[s], (s, t)).wait_recv()

    loads[1].wait()

    @pl.when(jnp.logical_not(far_slot))
    def _():
        meas_load.wait()

    @pl.when(far_slot)
    def _():
        meas_far.wait_recv()

    high, low = split(meas[...])
    high, low = split(dot(perm[...], high) + dot(perm[...], low))
    across = (((1,), (1,)), ((), ()))
    mp[...] = lax.dot_general(high, perm[...], across, preferred_element_type=F32) + lax.dot_general(
        low, perm[...], across, preferred_element_type=F32
    )
    loads[2].wait()

    def through(s, vr, vi):
        tr, ti = waves[s, 0], waves[s, 1]
        butterfly_store(tr * vr - ti * vi, tr * vi + ti * vr, dbuf)

    def forward(s, _):
        arrived(s)
        through(s, psi[s, 0], psi[s, 1])
        left_product(0, tab, dbuf, ebuf)
        o = unbutterfly(right_product(0, tab, ebuf))
        psi[s + 1, 0] = o[0]
        psi[s + 1, 1] = o[1]
        return 0

    lax.fori_loop(0, 3, forward, 0)
    arrived(3)
    through(3, psi[3, 0], psi[3, 1])
    left_product(1, tab, dbuf, ebuf)
    far = right_product(1, tab, ebuf)
    for b in range(2):
        fr, fi = far[b][:, :H], far[b][:, H:]
        excess = fr * fr + fi * fi - mp[:, half(b)]
        for c, z in ((0, excess * fr), (1, -(excess * fi))):
            for a in range(2):
                put(dbuf, a, half(c), half(b), z[half(a)])
    left_product(2, tab, dbuf, ebuf)
    o = unbutterfly(right_product(2, tab, ebuf))
    g[0] = o[0]
    g[1] = o[1]

    def g_copy(s):
        return remote(grads.at[s], grads_in.at[d], g_send.at[s], g_recv.at[d], (s, t))

    def contribute(s):
        pr, pi = psi[s, 0], psi[s, 1]
        gr, gi = g[0], g[1]
        grads[s, 0] = weight * (pr * gr - pi * gi)
        grads[s, 1] = -weight * (pr * gi + pi * gr)

        @pl.when(s != d)
        def _():
            g_copy(s).start()

    def backward(i, _):
        s = 3 - i
        contribute(s)
        through(s, g[0], g[1])
        left_product(0, tab, dbuf, ebuf)
        o = unbutterfly(right_product(0, tab, ebuf))
        g[0] = o[0]
        g[1] = o[1]
        return 0

    lax.fori_loop(0, 3, backward, 0)
    contribute(0)

    def spill_copy(src, k):
        to = jnp.where((odd == 1) & (k >= 2), tile(-1), tile(1))
        return remote(src, spill_out.at[k], spill_send.at[k], spill_recv.at[k], (d, to))

    def back_copy(src, k):
        return remote(src, own_out.at[k], back_send.at[k - 2], back_recv.at[k - 2], (d, tile(-2)))

    def own_copy(src, k):
        return pltpu.make_async_copy(src, own_out.at[k], out_sem.at[k])

    def place(src, k):
        spill_copy(src, k).start()

        @pl.when((odd == 1) & (k >= 2))
        def _():
            back_copy(src, k).start()

        @pl.when((odd == 0) | (k < 2))
        def _():
            own_copy(src, k).start()

    place(grads.at[d], d)
    for j in (1, 3, 2):
        k = level(j)
        remote(grads.at[0], grads_in.at[k], g_send.at[0], g_recv.at[k], (k, t)).wait_recv()
        place(grads_in.at[k], k)

    for r in range(2):
        for k in range(4):
            before_out[r, k] = pos1[r, k]

    for copy in infos:
        copy.wait_send()

    @pl.when(far_slot)
    def _():
        meas_far.wait_send()

    for k in range(4):
        halo_copy(k).wait_send()
        spill_copy(grads.at[0], k).wait()

        @pl.when(k != d)
        def _():
            y_copy(k).wait_send()
            g_copy(k).wait_send()

        if k < 2:
            own_copy(grads.at[0], k).wait()
        else:

            @pl.when(odd == 1)
            def _():
                far_copy(k).wait_send()
                back_copy(grads.at[0], k).wait()

            @pl.when(odd == 0)
            def _():
                own_copy(grads.at[0], k).wait()


def place_pieces(tiles, own, spill, positions, before, out, canvas, pieces, in_sem, out_sem):
    t = lax.axis_index("tile")
    loads = [pltpu.make_async_copy(own.at[k], pieces.at[k], in_sem.at[k]) for k in range(4)]
    loads += [pltpu.make_async_copy(spill.at[k], pieces.at[4 + k], in_sem.at[4 + k]) for k in range(4)]
    for copy in loads:
        copy.start()

    def clear(i, _):
        rows = pl.ds(pl.multiple_of(i * 8, 8), 8)
        for c in range(2):
            canvas[c, rows, :] = jnp.zeros((8, canvas.shape[2]), F32)
        return 0

    lax.fori_loop(0, N // 8, clear, 0)

    def add(k, row, col, top):
        block = lax.shift_right_logical(col, 7)
        rem = lax.bitwise_and(col, 127)
        odd = lax.bitwise_and(block, 1)
        chunk = 32

        def body(i, _):
            rows = pl.ds(pl.multiple_of(i * chunk, chunk), chunk)
            lane = lax.broadcasted_iota(jnp.int32, (chunk, H), 1)
            line = lax.broadcasted_iota(jnp.int32, (chunk, H), 0) + i * chunk
            keep = line >= row if top else line < row
            for c in range(2):
                same = pieces[k, c, rows, pl.ds(pl.multiple_of(odd * H, H), H)]
                other = pieces[k, c, rows, pl.ds(pl.multiple_of((1 - odd) * H, H), H)]
                for n, mask, x in ((0, keep & (lane >= rem), same), (1, keep, other), (2, keep & (lane < rem), same)):
                    cols = pl.ds(pl.multiple_of(jnp.minimum(block + n, 31) * H, H), H)
                    canvas[c, rows, cols] += jnp.where(mask, x, 0.0)
            return 0

        lax.fori_loop(0, N // chunk, body, 0)

    for k in range(4):
        loads[k].wait()
        add(k, positions[0, k] - t * N, positions[1, k], True)
    for k in range(4):
        loads[4 + k].wait()
        add(4 + k, before[0, k] - lax.rem(t + tiles - 1, tiles) * N, before[1, k], False)
    copy = pltpu.make_async_copy(canvas, out.at[:, 0], out_sem)
    copy.start()
    copy.wait()


def solution(mesh):
    depth, tiles = mesh.shape["depth"], mesh.shape["tile"]
    tables, order = transform_tables(), order_table()
    hbm = pl.BlockSpec(memory_space=pl.ANY)
    smem = pl.BlockSpec(memory_space=pltpu.SMEM)
    dma = pltpu.SemaphoreType.DMA

    def local(specimen, positions, occupied, measured, probe_wave):
        columns = specimen.shape[-1]
        own, spill, before = pl.pallas_call(
            functools.partial(gradient_pieces, depth, tiles),
            out_shape=(
                jax.ShapeDtypeStruct((4, *PIECE), F32),
                jax.ShapeDtypeStruct((4, *PIECE), F32),
                jax.ShapeDtypeStruct((2, 4), jnp.int32),
            ),
            in_specs=[hbm, smem, smem, hbm, hbm, hbm, hbm],
            out_specs=(hbm, hbm, smem),
            scratch_shapes=[
                pltpu.VMEM((columns // H, 2, N, H), F32),
                pltpu.VMEM((6, *PIECE), F32),
                pltpu.VMEM((4, *PIECE), F32),
                pltpu.VMEM((4, *PIECE), F32),
                pltpu.VMEM((4, *PIECE), F32),
                pltpu.VMEM((4, *PIECE), F32),
                pltpu.VMEM((4, *PIECE), F32),
                pltpu.VMEM(PIECE, F32),
                pltpu.VMEM((2, 2, N, N), BF),
                pltpu.VMEM((2, 2, N, N), BF),
                pltpu.VMEM((4, *PIECE), F32),
                pltpu.VMEM((4, *PIECE), F32),
                pltpu.VMEM(tables.shape, BF),
                pltpu.VMEM(order.shape, BF),
                pltpu.VMEM((N, N), F32),
                pltpu.VMEM((N, N), F32),
                pltpu.VMEM(PIECE, F32),
                pltpu.SMEM((2, 4), jnp.int32),
                pltpu.SMEM((2, 4), jnp.int32),
                pltpu.SMEM((4,), jnp.int32),
                dma((4,)), dma((columns // H,)), dma((3,)), dma((3,)), dma((4,)), dma((4,)), dma((2,)), dma((2,)),
                dma((4,)), dma((4,)), dma((4,)), dma((4,)), dma((4,)), dma((4,)), dma((2,)), dma((2,)),
                dma(()), dma(()), dma((4,)),
            ],
            compiler_params=pltpu.CompilerParams(
                collective_id=0, has_side_effects=True, vmem_limit_bytes=56 * 2**20
            ),
        )(specimen, positions, occupied, measured, probe_wave, tables, order)
        return pl.pallas_call(
            functools.partial(place_pieces, tiles),
            out_shape=jax.ShapeDtypeStruct(specimen.shape, F32),
            in_specs=[hbm, hbm, smem, smem],
            out_specs=hbm,
            scratch_shapes=[
                pltpu.VMEM((2, N, columns), F32),
                pltpu.VMEM((8, *PIECE), F32),
                dma((8,)),
                dma(()),
            ],
            compiler_params=pltpu.CompilerParams(vmem_limit_bytes=32 * 2**20),
        )(own, spill, positions, before)

    return jax.shard_map(
        local,
        mesh=mesh,
        in_specs=(P(None, "depth", "tile", None), P(None, "tile"), P("tile"), P("tile", None, None), P()),
        out_specs=P(None, "depth", "tile", None),
        check_vma=False,
    )
```

```python
import functools
import math

import jax
import jax.numpy as jnp
import ml_dtypes
import numpy as np
from jax import lax
from jax.experimental import pallas as pl
from jax.experimental.pallas import tpu as pltpu
from jax.sharding import PartitionSpec as P

MESH = pl.DeviceIdType.MESH
BF = jnp.bfloat16
F32 = jnp.float32
N = 256
H = 128
PIECE = (2, N, N)


def transform_tables():
    j = np.arange(N)
    unitary = np.exp(-2j * np.pi * ((j[:, None] * j[None, :]) % N) / N) / math.sqrt(N)
    f = ((j + H) % N) - H
    kernel = np.conj(unitary) @ (np.exp(-12j * f * f / (N * N))[:, None] * unitary)
    kernels = [(kernel[:H, :H] + sign * kernel[:H, H:]) / 2 for sign in (1, -1)]
    halves = [unitary[:H, 0::2], unitary[:H, 1::2]]

    def left(m):
        return np.block([[m.real, -m.imag], [m.imag, m.real]])

    def right(m):
        return np.block([[m.real, m.imag], [-m.imag, m.real]])

    lefts = [[left(m) for m in kernels], [left(m.T) for m in halves], [left(m) for m in halves]]
    rights = [[right(m) for m in kernels], [right(m) for m in halves], [right(m.T) for m in halves]]
    exact = np.array([lefts, rights])
    high = exact.astype(ml_dtypes.bfloat16)
    low = (exact - high.astype(np.float64)).astype(ml_dtypes.bfloat16)
    return np.stack([high, low], axis=3)


def order_table():
    table = np.zeros((N, N))
    table[np.arange(N), np.r_[0:N:2, 1:N:2]] = 1
    return table.astype(ml_dtypes.bfloat16)


def split(x):
    high = x.astype(BF)
    return high, (x - high.astype(F32)).astype(BF)


def dot(a, b):
    return jnp.dot(a, b, preferred_element_type=F32)


def exact_dot(multiply, x):
    high = x.astype(BF)
    rest = x - high.astype(F32)
    middle = rest.astype(BF)
    low = (rest - middle.astype(F32)).astype(BF)
    return multiply(high) + (multiply(middle) + multiply(low))


def put(buf, index, rows, cols, x):
    high, low = split(x)
    buf[index, 0, rows, cols] = high
    buf[index, 1, rows, cols] = low


def half(i):
    return slice(i * H, (i + 1) * H)


def butterfly_store(xr, xi, dbuf):
    for c, x in ((0, xr), (1, xi)):
        top, bottom = x[:H], x[H:]
        for a, y in ((0, top + bottom), (1, top - bottom)):
            put(dbuf, a, half(c), half(0), y[:, :H] + y[:, H:])
            put(dbuf, a, half(c), half(1), y[:, :H] - y[:, H:])


def left_product(kind, tab, dbuf, ebuf):
    for a in range(2):
        high, low = dbuf[a, 0], dbuf[a, 1]
        e = dot(tab[0, kind, a, 0], high) + (dot(tab[0, kind, a, 0], low) + dot(tab[0, kind, a, 1], high))
        for c in range(2):
            for b in range(2):
                put(ebuf, b, half(a), half(c), e[half(c), half(b)])


def right_product(kind, tab, ebuf):
    out = []
    for b in range(2):
        high, low = ebuf[b, 0], ebuf[b, 1]
        out.append(dot(high, tab[1, kind, b, 0]) + (dot(low, tab[1, kind, b, 0]) + dot(high, tab[1, kind, b, 1])))
    return out


def unbutterfly(g):
    res = []
    for c in range(2):
        p, m = g[0][:, half(c)], g[1][:, half(c)]
        y = jnp.concatenate([p + m, p - m], axis=1)
        res.append(jnp.concatenate([y[:H] + y[H:], y[:H] - y[H:]], axis=0))
    return res


def cut(spec, row, col, top, store):
    block = lax.div(col, H)
    rem = lax.rem(col, H)
    odd = lax.rem(block, 2)
    chunk = 32

    def body(i, _):
        rows = pl.ds(pl.multiple_of(i * chunk, chunk), chunk)
        lane = lax.broadcasted_iota(jnp.int32, (chunk, H), 1)
        line = lax.broadcasted_iota(jnp.int32, (chunk, H), 0) + i * chunk
        keep = line >= row if top else line < row
        for side in range(2):
            first = block + (odd if side == 0 else 1 - odd)
            second = first + 2 - 2 * lax.div(first + 2, 32)
            limit = rem * (1 - odd if side == 0 else odd)
            for c in range(2):
                here = spec[first, c, rows, :]
                there = spec[second, c, rows, :]
                store(c, rows, half(side), jnp.where(keep, jnp.where(lane >= limit, here, there), 0.0))
        return 0

    lax.fori_loop(0, N // chunk, body, 0)


def add_pieces(canvas, pool, pieces):
    chunk = 16

    def body(i, _):
        rows = pl.ds(pl.multiple_of(i * chunk, chunk), chunk)
        lane = lax.broadcasted_iota(jnp.int32, (chunk, H), 1)
        line = lax.broadcasted_iota(jnp.int32, (chunk, H), 0) + i * chunk
        keeps = [line >= row if top else line < row for _, row, _, top in pieces]
        for c in range(2):
            values = [
                [jnp.where(keep, pool[slot, c, rows, half(h)], 0.0) for h in range(2)]
                for keep, (slot, _, _, _) in zip(keeps, pieces)
            ]
            for b in range(canvas.shape[2] // H):
                total = canvas[c, rows, half(b)]
                for value, (_, _, col, _) in zip(values, pieces):
                    at = lane + (b * H - col)
                    total += jnp.where((at >= 0) & (at < N), value[b % 2], 0.0)
                canvas[c, rows, half(b)] = total
        return 0

    lax.fori_loop(0, N // chunk, body, 0)


def gradient_kernel(
    depth, tiles, specimen, positions, occupied, measured, probe, tables, order, canvas,
    spec, mine, halo_out, halo_in, merged, waves, psi, g, dbuf, ebuf, pool, tab, perm, meas, mp,
    wave0, pos0, pos1, pos2,
    load_sem, spec_sem, info_send, info_recv, halo_send, halo_recv, far_send, far_recv, y_send, y_recv,
    g_send, g_recv, spill_send, spill_recv, back_send, back_recv, meas_send, meas_recv, turn_sem,
):
    d = lax.axis_index("depth")
    t = lax.axis_index("tile")
    odd = lax.rem(t, 2)
    both = range(2)

    def tile(k):
        return lax.rem(t + k + tiles, tiles)

    def level(k):
        return lax.rem(d + k, depth)

    def remote(src, dst, send, recv, to):
        return pltpu.make_async_remote_copy(
            src_ref=src, dst_ref=dst, send_sem=send, recv_sem=recv, device_id=to, device_id_type=MESH
        )

    near = lax.rem(d + 1, 2)
    turns = (near, near + 2, level(2), d)
    far_slot = (odd == 1) & (d >= 2)

    probe_load = pltpu.make_async_copy(probe, wave0, load_sem.at[0])
    order_load = pltpu.make_async_copy(order, perm, load_sem.at[1])
    tables_load = pltpu.make_async_copy(tables, tab, load_sem.at[2])
    meas_load = pltpu.make_async_copy(measured.at[d], meas, load_sem.at[3])
    blocks = spec.shape[0]

    def block_load(b):
        cols = pl.ds(pl.multiple_of(b * H, H), H)
        return pltpu.make_async_copy(specimen.at[:, 0, :, cols], spec.at[b], spec_sem.at[b])

    lax.fori_loop(0, blocks, lambda b, _: (block_load(b).start(), 0)[1], 0)
    probe_load.start()
    order_load.start()

    @pl.when(jnp.logical_not(far_slot))
    def _():
        meas_load.start()

    tables_load.start()

    barrier = pltpu.get_barrier_semaphore()
    partners = [(level(k), t) for k in range(1, 4)] + [(d, tile(k)) for k in (-1, 1)]
    wide = [(d, tile(k)) for k in (-2, 2)]
    for partner in partners:
        pl.semaphore_signal(barrier, inc=1, device_id=partner, device_id_type=MESH)

    @pl.when(odd == 1)
    def _():
        for partner in wide:
            pl.semaphore_signal(barrier, inc=1, device_id=partner, device_id_type=MESH)

    for k in range(4):
        pos0[0, k] = (positions[0, k] - t * N) * occupied[k]
        pos0[1, k] = positions[1, k]

    def cut_top(k):
        def store(c, rows, cols, x):
            mine[k, c, rows, cols] = x

        cut(spec, pos0[0, k] + N * (1 - occupied[k]), pos0[1, k], True, store)

    def turn_probe(row, col):
        line = lax.broadcasted_iota(jnp.int32, (N, N), 0)
        lane = lax.broadcasted_iota(jnp.int32, (N, N), 1)
        turn_rows = (lax.bitwise_and(line - lane - row, N - 1) == 0).astype(F32).astype(BF)
        turn_cols = (lax.bitwise_and(lane - line - col, N - 1) == 0).astype(F32).astype(BF)
        for c in both:
            turned = exact_dot(lambda x: dot(turn_rows, x), wave0[c])
            psi[0, c] = exact_dot(lambda x: dot(x, turn_cols), turned)

    def order_measured():
        high, low = split(meas[...])
        high, low = split(dot(perm[...], high) + dot(perm[...], low))
        across = (((1,), (1,)), ((), ()))
        mp[...] = lax.dot_general(high, perm[...], across, preferred_element_type=F32) + lax.dot_general(
            low, perm[...], across, preferred_element_type=F32
        )

    def clear(i, _):
        rows = pl.ds(pl.multiple_of(i * 8, 8), 8)
        for c in both:
            canvas[c, rows, :] = jnp.zeros((8, canvas.shape[2]), F32)
        return 0

    pl.semaphore_wait(barrier, jnp.where(odd == 1, len(partners) + len(wide), len(partners)))

    info1 = remote(pos0, pos1, info_send.at[0], info_recv.at[0], (d, tile(1)))
    info2 = remote(pos0, pos2, info_send.at[1], info_recv.at[1], (d, tile(2)))
    meas_far = remote(measured.at[d], meas, meas_send, meas_recv, (d, tile(2)))

    def far_copy(k, c):
        return remote(mine.at[k, c], mine.at[k + 2, c], far_send.at[k - 2, c], far_recv.at[k - 2, c], (d, tile(2)))

    def halo_copy(k, c):
        to = jnp.where((odd == 1) | (k < 2), tile(-1), tile(1))
        return remote(halo_out.at[k, c], halo_in.at[k, c], halo_send.at[k, c], halo_recv.at[k, c], (d, to))

    info1.start()

    @pl.when(odd == 1)
    def _():
        info2.start()

    lax.fori_loop(0, blocks, lambda b, _: (block_load(b).wait(), 0)[1], 0)

    @pl.when(odd == 1)
    def _():
        for k in (near + 2, 3 - near):
            cut_top(k)
            for c in both:
                far_copy(k, c).start()

    @pl.when(far_slot)
    def _():
        meas_far.start()

    info1.wait_recv()

    def cut_bottom(k):
        def store(c, rows, cols, x):
            halo_out[k, c, rows, cols] = x

        cut(spec, pos1[0, k], pos1[1, k], False, store)
        for c in both:
            halo_copy(k, c).start()

    for k in turns:
        cut_bottom(k)
    for k in turns:

        @pl.when((odd == 0) | (k < 2))
        def _():
            cut_top(k)

    def y_copy(k, c):
        return remote(merged.at[k, c], waves.at[d, c], y_send.at[k, c], y_recv.at[d, c], (k, t))

    def merge(k, c, dst):
        halo_copy(k, c).wait_recv()

        @pl.when((odd == 1) & (k >= 2))
        def _():
            far_copy(k, c).wait_recv()

        source = jnp.where((odd == 1) & (k >= 2), k + 2, k)

        def body(i, _):
            rows = pl.ds(pl.multiple_of(i * 64, 64), 64)
            dst[c, rows, :] = mine[source, c, rows, :] + halo_in[k, c, rows, :]
            return 0

        lax.fori_loop(0, N // 64, body, 0)

    def merge_level(k):
        for c in both:
            merge(k, c, merged.at[k])

    def send_level(k):
        for c in both:
            y_copy(k, c).start()

    merge_level(turns[0])
    merge_level(turns[1])

    @pl.when(odd == 0)
    def _():
        send_level(turns[0])
        send_level(turns[1])
        merge_level(turns[2])
        send_level(turns[2])

    @pl.when(odd == 1)
    def _():
        info2.wait_recv()

    probe_load.wait()
    turn_probe(jnp.where(far_slot, pos2[0, d], pos0[0, d]), jnp.where(far_slot, pos2[1, d], pos0[1, d]))
    lax.fori_loop(0, N // 8, clear, 0)

    @pl.when(odd == 1)
    def _():
        pl.semaphore_wait(turn_sem.at[0], 1)
        send_level(turns[0])
        send_level(turns[1])
        merge_level(turns[2])
        send_level(turns[2])

    for c in both:
        merge(d, c, waves.at[d])

    @pl.when(odd == 0)
    def _():
        for k in turns[:2]:
            for c in both:
                y_copy(k, c).wait_send()
        y_copy(turns[2], 0).wait_send()
        pl.semaphore_signal(turn_sem.at[0], inc=1, device_id=(d, t + 1), device_id_type=MESH)

    order_load.wait()

    @pl.when(far_slot)
    def _():
        meas_far.wait_recv()

    @pl.when(jnp.logical_not(far_slot))
    def _():
        meas_load.wait()

    order_measured()
    tables_load.wait()

    def arrived(s):
        @pl.when(s != d)
        def _():
            for c in both:
                remote(merged.at[0, c], waves.at[s, c], y_send.at[0, c], y_recv.at[s, c], (s, t)).wait_recv()

    def through(s, vr, vi):
        tr, ti = waves[s, 0], waves[s, 1]
        butterfly_store(tr * vr - ti * vi, tr * vi + ti * vr, dbuf)

    def forward(s, _):
        arrived(s)
        through(s, psi[s, 0], psi[s, 1])
        left_product(0, tab, dbuf, ebuf)
        o = unbutterfly(right_product(0, tab, ebuf))
        psi[s + 1, 0] = o[0]
        psi[s + 1, 1] = o[1]
        return 0

    lax.fori_loop(0, 3, forward, 0)
    arrived(3)

    through(3, psi[3, 0], psi[3, 1])
    left_product(1, tab, dbuf, ebuf)
    far = right_product(1, tab, ebuf)
    for b in both:
        fr, fi = far[b][:, :H], far[b][:, H:]
        excess = fr * fr + fi * fi - mp[:, half(b)]
        for c, z in ((0, excess * fr), (1, -(excess * fi))):
            for a in both:
                put(dbuf, a, half(c), half(b), z[half(a)])
    left_product(2, tab, dbuf, ebuf)
    o = unbutterfly(right_product(2, tab, ebuf))
    g[0] = o[0]
    g[1] = o[1]

    def g_copy(s, c):
        return remote(pool.at[s + 6, c], pool.at[d, c], g_send.at[s, c], g_recv.at[d, c], (s, t))

    def contribute(s):
        slot = jnp.where(s == d, d, s + 6)
        pr, pi = psi[s, 0], psi[s, 1]
        gr, gi = g[0], g[1]
        pool[slot, 0] = pr * gr - pi * gi
        pool[slot, 1] = -(pr * gi + pi * gr)

    def backward(i, _):
        s = 3 - i
        contribute(s)
        through(s, g[0], g[1])
        left_product(0, tab, dbuf, ebuf)
        o = unbutterfly(right_product(0, tab, ebuf))
        g[0] = o[0]
        g[1] = o[1]
        return 0

    lax.fori_loop(0, 3, backward, 0)
    contribute(0)

    def spill_copy(k, c):
        to = jnp.where((odd == 1) & (k >= 2), tile(-1), tile(1))
        return remote(pool.at[k, c], pool.at[k + 10, c], spill_send.at[k, c], spill_recv.at[k, c], (d, to))

    def back_copy(k, c):
        return remote(pool.at[k, c], pool.at[k + 2, c], back_send.at[k - 2, c], back_recv.at[k - 2, c], (d, tile(-2)))

    def send_back(k, c):
        g_copy(k, c).start()

    def pass_on(k):
        for c in both:

            @pl.when(k != d)
            def _():
                remote(pool.at[6, c], pool.at[k, c], g_send.at[0, c], g_recv.at[k, c], (k, t)).wait_recv()

            @pl.when((odd == 1) & (k >= 2))
            def _():
                back_copy(k, c).start()

            spill_copy(k, c).start()

    def mine_of(k):
        @pl.when((odd == 1) & (k >= 2))
        def _():
            for c in both:
                back_copy(k, c).wait_recv()

        return (jnp.where((odd == 1) & (k >= 2), k + 2, k), pos0[0, k], pos0[1, k], True)

    def spilled_of(k):
        for c in both:
            spill_copy(k, c).wait_recv()
        return (k + 10, pos1[0, k], pos1[1, k], False)

    first, second, across = turns[:3]

    @pl.when(odd == 0)
    def _():
        for c in both:
            send_back(first, c)
            send_back(second, c)
        send_back(across, 0)

    @pl.when(odd == 1)
    def _():
        for c in both:
            send_back(first, c)
            send_back(second, c)

    pass_on(d)

    @pl.when(odd == 1)
    def _():
        for c in both:
            g_copy(first, c).wait_send()
            g_copy(second, c).wait_send()
        for c in both:
            send_back(across, c)

    pass_on(first)
    pass_on(second)

    @pl.when(odd == 0)
    def _():
        add_pieces(canvas, pool, [mine_of(d)])
        add_pieces(canvas, pool, [mine_of(first), mine_of(second)])
        pl.semaphore_wait(turn_sem.at[1], 1)
        send_back(across, 1)
        add_pieces(canvas, pool, [spilled_of(d), spilled_of(first), spilled_of(second)])
        pass_on(across)

    @pl.when(odd == 1)
    def _():
        add_pieces(canvas, pool, [mine_of(d)])
        g_copy(across, 0).wait_send()
        pl.semaphore_signal(turn_sem.at[1], inc=1, device_id=(d, t - 1), device_id_type=MESH)
        add_pieces(canvas, pool, [spilled_of(d), spilled_of(first), spilled_of(second)])
        pass_on(across)
        add_pieces(canvas, pool, [mine_of(first), mine_of(second)])

    add_pieces(canvas, pool, [mine_of(across), spilled_of(across)])

    info1.wait_send()

    @pl.when(far_slot)
    def _():
        meas_far.wait_send()

    @pl.when(odd == 1)
    def _():
        info2.wait_send()
        for c in both:
            for k in (2, 3):
                far_copy(k, c).wait_send()
                back_copy(k, c).wait_send()
            y_copy(first, c).wait_send()
            y_copy(second, c).wait_send()
        y_copy(across, 0).wait_send()
        g_copy(across, 1).wait_send()

    @pl.when(odd == 0)
    def _():
        for c in both:
            for k in (first, second, across):
                g_copy(k, c).wait_send()

    y_copy(across, 1).wait_send()
    for k in range(4):
        for c in both:
            halo_copy(k, c).wait_send()
            spill_copy(k, c).wait_send()


def solution(mesh):
    depth, tiles = mesh.shape["depth"], mesh.shape["tile"]
    tables, order = transform_tables(), order_table()
    hbm = pl.BlockSpec(memory_space=pl.ANY)
    smem = pl.BlockSpec(memory_space=pltpu.SMEM)
    dma = pltpu.SemaphoreType.DMA

    def pieces(count):
        return pltpu.VMEM((count, *PIECE), F32)

    def local(specimen, positions, occupied, measured, probe_wave):
        columns = specimen.shape[-1]
        canvas = pl.pallas_call(
            functools.partial(gradient_kernel, depth, tiles),
            out_shape=pltpu.VMEM((2, N, columns), F32),
            in_specs=[hbm, smem, smem, hbm, hbm, hbm, hbm],
            out_specs=pl.BlockSpec(memory_space=pltpu.VMEM),
            scratch_shapes=[
                pltpu.VMEM((columns // H, 2, N, H), F32),
                pieces(6), pieces(4), pieces(4), pieces(4), pieces(4), pieces(4),
                pltpu.VMEM(PIECE, F32),
                pltpu.VMEM((2, 2, N, N), BF),
                pltpu.VMEM((2, 2, N, N), BF),
                pieces(14),
                pltpu.VMEM(tables.shape, BF),
                pltpu.VMEM(order.shape, BF),
                pltpu.VMEM((N, N), F32),
                pltpu.VMEM((N, N), F32),
                pltpu.VMEM(PIECE, F32),
                pltpu.SMEM((2, 4), jnp.int32),
                pltpu.SMEM((2, 4), jnp.int32),
                pltpu.SMEM((2, 4), jnp.int32),
                dma((4,)), dma((columns // H,)), dma((2,)), dma((2,)), dma((4, 2)), dma((4, 2)), dma((2, 2)), dma((2, 2)),
                dma((4, 2)), dma((4, 2)), dma((4, 2)), dma((4, 2)), dma((4, 2)), dma((4, 2)), dma((2, 2)), dma((2, 2)),
                dma(()), dma(()), pltpu.SemaphoreType.REGULAR((2,)),
            ],
            compiler_params=pltpu.CompilerParams(
                collective_id=0, has_side_effects=True, vmem_limit_bytes=48 * 2**20
            ),
        )(specimen, positions, occupied, measured, probe_wave, tables, order)
        return canvas[:, None]

    return jax.shard_map(
        local,
        mesh=mesh,
        in_specs=(P(None, "depth", "tile", None), P(None, "tile"), P("tile"), P("tile", None, None), P()),
        out_specs=P(None, "depth", "tile", None),
        check_vma=False,
    )
```

```python
import functools
import math

import jax
import jax.numpy as jnp
import ml_dtypes
import numpy as np
from jax import lax
from jax.experimental import pallas as pl
from jax.experimental.pallas import tpu as pltpu
from jax.sharding import PartitionSpec as P

MESH = pl.DeviceIdType.MESH
BF = jnp.bfloat16
F32 = jnp.float32
N = 256
H = 128
PIECE = (2, N, N)


def transform_tables():
    j = np.arange(N)
    unitary = np.exp(-2j * np.pi * ((j[:, None] * j[None, :]) % N) / N) / math.sqrt(N)
    f = ((j + H) % N) - H
    kernel = np.conj(unitary) @ (np.exp(-12j * f * f / (N * N))[:, None] * unitary)
    kernels = [(kernel[:H, :H] + sign * kernel[:H, H:]) / 2 for sign in (1, -1)]
    halves = [unitary[:H, 0::2], unitary[:H, 1::2]]

    def left(m):
        return np.block([[m.real, -m.imag], [m.imag, m.real]])

    def right(m):
        return np.block([[m.real, m.imag], [-m.imag, m.real]])

    lefts = [[left(m) for m in kernels], [left(m.T) for m in halves], [left(m) for m in halves]]
    rights = [[right(m) for m in kernels], [right(m) for m in halves], [right(m.T) for m in halves]]
    exact = np.array([lefts, rights])
    high = exact.astype(ml_dtypes.bfloat16)
    low = (exact - high.astype(np.float64)).astype(ml_dtypes.bfloat16)
    return np.stack([high, low], axis=3)


def order_table():
    table = np.zeros((N, N))
    table[np.arange(N), np.r_[0:N:2, 1:N:2]] = 1
    return table.astype(ml_dtypes.bfloat16)


def split(x):
    high = x.astype(BF)
    return high, (x - high.astype(F32)).astype(BF)


def dot(a, b):
    return jnp.dot(a, b, preferred_element_type=F32)


def exact_dot(multiply, x):
    high = x.astype(BF)
    rest = x - high.astype(F32)
    middle = rest.astype(BF)
    low = (rest - middle.astype(F32)).astype(BF)
    return multiply(high) + (multiply(middle) + multiply(low))


def put(buf, index, rows, cols, x):
    high, low = split(x)
    buf[index, 0, rows, cols] = high
    buf[index, 1, rows, cols] = low


def half(i):
    return slice(i * H, (i + 1) * H)


def butterfly_store(xr, xi, dbuf):
    for c, x in ((0, xr), (1, xi)):
        top, bottom = x[:H], x[H:]
        for a, y in ((0, top + bottom), (1, top - bottom)):
            put(dbuf, a, half(c), half(0), y[:, :H] + y[:, H:])
            put(dbuf, a, half(c), half(1), y[:, :H] - y[:, H:])


def left_product(kind, tab, dbuf, ebuf):
    for a in range(2):
        high, low = dbuf[a, 0], dbuf[a, 1]
        e = dot(tab[0, kind, a, 0], high) + (dot(tab[0, kind, a, 0], low) + dot(tab[0, kind, a, 1], high))
        for c in range(2):
            for b in range(2):
                put(ebuf, b, half(a), half(c), e[half(c), half(b)])


def right_product(kind, tab, ebuf):
    out = []
    for b in range(2):
        high, low = ebuf[b, 0], ebuf[b, 1]
        out.append(dot(high, tab[1, kind, b, 0]) + (dot(low, tab[1, kind, b, 0]) + dot(high, tab[1, kind, b, 1])))
    return out


def unbutterfly(g):
    res = []
    for c in range(2):
        p, m = g[0][:, half(c)], g[1][:, half(c)]
        y = jnp.concatenate([p + m, p - m], axis=1)
        res.append(jnp.concatenate([y[:H] + y[H:], y[:H] - y[H:]], axis=0))
    return res


def cut(spec, row, col, top, store):
    block = lax.div(col, H)
    rem = lax.rem(col, H)
    odd = lax.rem(block, 2)
    chunk = 32

    def body(i, _):
        rows = pl.ds(pl.multiple_of(i * chunk, chunk), chunk)
        lane = lax.broadcasted_iota(jnp.int32, (chunk, H), 1)
        line = lax.broadcasted_iota(jnp.int32, (chunk, H), 0) + i * chunk
        keep = line >= row if top else line < row
        for side in range(2):
            first = block + (odd if side == 0 else 1 - odd)
            second = first + 2 - 2 * lax.div(first + 2, 32)
            limit = rem * (1 - odd if side == 0 else odd)
            for c in range(2):
                here = spec[first, c, rows, :]
                there = spec[second, c, rows, :]
                store(c, rows, half(side), jnp.where(keep, jnp.where(lane >= limit, here, there), 0.0))
        return 0

    lax.fori_loop(0, N // chunk, body, 0)


def add_pieces(canvas, pool, pieces, parts=(0, 1)):
    chunk = 16

    def body(i, _):
        rows = pl.ds(pl.multiple_of(i * chunk, chunk), chunk)
        lane = lax.broadcasted_iota(jnp.int32, (chunk, H), 1)
        line = lax.broadcasted_iota(jnp.int32, (chunk, H), 0) + i * chunk
        keeps = [line >= row if top else line < row for _, row, _, top in pieces]
        for c in parts:
            values = [
                [jnp.where(keep, pool[slot, c, rows, half(h)], 0.0) for h in range(2)]
                for keep, (slot, _, _, _) in zip(keeps, pieces)
            ]
            for b in range(canvas.shape[2] // H):
                total = canvas[c, rows, half(b)]
                for value, (_, _, col, _) in zip(values, pieces):
                    at = lane + (b * H - col)
                    total += jnp.where((at >= 0) & (at < N), value[b % 2], 0.0)
                canvas[c, rows, half(b)] = total
        return 0

    lax.fori_loop(0, N // chunk, body, 0)


def gradient_kernel(
    depth, tiles, specimen, positions, occupied, measured, probe, tables, order, canvas,
    spec, mine, halo_out, halo_in, merged, waves, psi, g, dbuf, ebuf, pool, tab, perm, meas, mp,
    wave0, pos0, pos1, pos2,
    load_sem, spec_sem, info_send, info_recv, halo_send, halo_recv, far_send, far_recv, y_send, y_recv,
    g_send, g_recv, spill_send, spill_recv, back_send, back_recv, meas_send, meas_recv, turn_sem,
):
    d = lax.axis_index("depth")
    t = lax.axis_index("tile")
    odd = lax.rem(t, 2)
    both = range(2)

    def tile(k):
        return lax.rem(t + k + tiles, tiles)

    def level(k):
        return lax.rem(d + k, depth)

    def remote(src, dst, send, recv, to):
        return pltpu.make_async_remote_copy(
            src_ref=src, dst_ref=dst, send_sem=send, recv_sem=recv, device_id=to, device_id_type=MESH
        )

    near = lax.rem(d + 1, 2)
    turns = (near, near + 2, level(2), d)
    far_slot = (odd == 1) & (d >= 2)

    probe_load = pltpu.make_async_copy(probe, wave0, load_sem.at[0])
    order_load = pltpu.make_async_copy(order, perm, load_sem.at[1])
    tables_load = pltpu.make_async_copy(tables, tab, load_sem.at[2])
    meas_load = pltpu.make_async_copy(measured.at[d], meas, load_sem.at[3])
    blocks = spec.shape[0]

    def block_load(b):
        cols = pl.ds(pl.multiple_of(b * H, H), H)
        return pltpu.make_async_copy(specimen.at[:, 0, :, cols], spec.at[b], spec_sem.at[b])

    lax.fori_loop(0, blocks, lambda b, _: (block_load(b).start(), 0)[1], 0)
    probe_load.start()
    order_load.start()

    @pl.when(jnp.logical_not(far_slot))
    def _():
        meas_load.start()

    tables_load.start()

    barrier = pltpu.get_barrier_semaphore()
    partners = [(level(k), t) for k in range(1, 4)] + [(d, tile(k)) for k in (-1, 1)]
    wide = [(d, tile(k)) for k in (-2, 2)]
    for partner in partners:
        pl.semaphore_signal(barrier, inc=1, device_id=partner, device_id_type=MESH)

    @pl.when(odd == 1)
    def _():
        for partner in wide:
            pl.semaphore_signal(barrier, inc=1, device_id=partner, device_id_type=MESH)

    for k in range(4):
        pos0[0, k] = (positions[0, k] - t * N) * occupied[k]
        pos0[1, k] = positions[1, k]

    def cut_top(k):
        def store(c, rows, cols, x):
            mine[k, c, rows, cols] = x

        cut(spec, pos0[0, k] + N * (1 - occupied[k]), pos0[1, k], True, store)

    def turn_probe(row, col):
        line = lax.broadcasted_iota(jnp.int32, (N, N), 0)
        lane = lax.broadcasted_iota(jnp.int32, (N, N), 1)
        turn_rows = (lax.bitwise_and(line - lane - row, N - 1) == 0).astype(F32).astype(BF)
        turn_cols = (lax.bitwise_and(lane - line - col, N - 1) == 0).astype(F32).astype(BF)
        for c in both:
            turned = exact_dot(lambda x: dot(turn_rows, x), wave0[c])
            psi[0, c] = exact_dot(lambda x: dot(x, turn_cols), turned)

    def order_measured():
        high, low = split(meas[...])
        high, low = split(dot(perm[...], high) + dot(perm[...], low))
        across = (((1,), (1,)), ((), ()))
        mp[...] = lax.dot_general(high, perm[...], across, preferred_element_type=F32) + lax.dot_general(
            low, perm[...], across, preferred_element_type=F32
        )

    def clear(i, _):
        rows = pl.ds(pl.multiple_of(i * 8, 8), 8)
        for c in both:
            canvas[c, rows, :] = jnp.zeros((8, canvas.shape[2]), F32)
        return 0

    pl.semaphore_wait(barrier, jnp.where(odd == 1, len(partners) + len(wide), len(partners)))

    info1 = remote(pos0, pos1, info_send.at[0], info_recv.at[0], (d, tile(1)))
    info2 = remote(pos0, pos2, info_send.at[1], info_recv.at[1], (d, tile(2)))
    meas_far = remote(measured.at[d], meas, meas_send, meas_recv, (d, tile(2)))

    def far_copy(k, c):
        return remote(mine.at[k, c], mine.at[k + 2, c], far_send.at[k - 2, c], far_recv.at[k - 2, c], (d, tile(2)))

    def halo_copy(k, c):
        to = jnp.where((odd == 1) | (k < 2), tile(-1), tile(1))
        return remote(halo_out.at[k, c], halo_in.at[k, c], halo_send.at[k, c], halo_recv.at[k, c], (d, to))

    info1.start()

    @pl.when(odd == 1)
    def _():
        info2.start()

    lax.fori_loop(0, blocks, lambda b, _: (block_load(b).wait(), 0)[1], 0)

    info1.wait_recv()

    def cut_bottom(k):
        def store(c, rows, cols, x):
            halo_out[k, c, rows, cols] = x

        cut(spec, pos1[0, k], pos1[1, k], False, store)
        for c in both:
            halo_copy(k, c).start()

    def cut_mine(k):
        @pl.when((odd == 0) | (k < 2))
        def _():
            cut_top(k)

    cut_bottom(turns[0])
    cut_bottom(turns[1])

    @pl.when(odd == 1)
    def _():
        for k in (near + 2, 3 - near):
            cut_top(k)
            for c in both:
                far_copy(k, c).start()

    @pl.when(far_slot)
    def _():
        meas_far.start()

    cut_bottom(turns[2])
    cut_bottom(turns[3])
    cut_mine(turns[0])
    cut_mine(turns[1])

    def y_copy(k, c):
        return remote(merged.at[k, c], waves.at[d, c], y_send.at[k, c], y_recv.at[d, c], (k, t))

    def merge(k, c, dst):
        halo_copy(k, c).wait_recv()

        @pl.when((odd == 1) & (k >= 2))
        def _():
            far_copy(k, c).wait_recv()

        source = jnp.where((odd == 1) & (k >= 2), k + 2, k)

        def body(i, _):
            rows = pl.ds(pl.multiple_of(i * 64, 64), 64)
            dst[c, rows, :] = mine[source, c, rows, :] + halo_in[k, c, rows, :]
            return 0

        lax.fori_loop(0, N // 64, body, 0)

    def merge_level(k):
        for c in both:
            merge(k, c, merged.at[k])

    def send_level(k):
        for c in both:
            y_copy(k, c).start()

    merge_level(turns[0])
    merge_level(turns[1])

    @pl.when(odd == 0)
    def _():
        send_level(turns[0])
        send_level(turns[1])
        cut_mine(turns[2])
        merge_level(turns[2])
        send_level(turns[2])
        cut_mine(turns[3])

    @pl.when(odd == 1)
    def _():
        cut_mine(turns[2])
        cut_mine(turns[3])

    @pl.when(odd == 1)
    def _():
        info2.wait_recv()

    probe_load.wait()
    turn_probe(jnp.where(far_slot, pos2[0, d], pos0[0, d]), jnp.where(far_slot, pos2[1, d], pos0[1, d]))
    lax.fori_loop(0, N // 8, clear, 0)

    @pl.when(odd == 1)
    def _():
        pl.semaphore_wait(turn_sem.at[0], 1)
        send_level(turns[0])
        send_level(turns[1])
        merge_level(turns[2])
        send_level(turns[2])

    for c in both:
        merge(d, c, waves.at[d])

    @pl.when(odd == 0)
    def _():
        for k in turns[:2]:
            for c in both:
                y_copy(k, c).wait_send()
        y_copy(turns[2], 0).wait_send()
        pl.semaphore_signal(turn_sem.at[0], inc=1, device_id=(d, t + 1), device_id_type=MESH)

    order_load.wait()

    @pl.when(far_slot)
    def _():
        meas_far.wait_recv()

    @pl.when(jnp.logical_not(far_slot))
    def _():
        meas_load.wait()

    order_measured()
    tables_load.wait()

    def arrived(s):
        @pl.when(s != d)
        def _():
            for c in both:
                remote(merged.at[0, c], waves.at[s, c], y_send.at[0, c], y_recv.at[s, c], (s, t)).wait_recv()

    def through(s, vr, vi):
        tr, ti = waves[s, 0], waves[s, 1]
        butterfly_store(tr * vr - ti * vi, tr * vi + ti * vr, dbuf)

    def forward(s, _):
        arrived(s)
        through(s, psi[s, 0], psi[s, 1])
        left_product(0, tab, dbuf, ebuf)
        o = unbutterfly(right_product(0, tab, ebuf))
        psi[s + 1, 0] = o[0]
        psi[s + 1, 1] = o[1]
        return 0

    lax.fori_loop(0, 3, forward, 0)
    arrived(3)

    through(3, psi[3, 0], psi[3, 1])
    left_product(1, tab, dbuf, ebuf)
    far = right_product(1, tab, ebuf)
    for b in both:
        fr, fi = far[b][:, :H], far[b][:, H:]
        excess = fr * fr + fi * fi - mp[:, half(b)]
        for c, z in ((0, excess * fr), (1, -(excess * fi))):
            for a in both:
                put(dbuf, a, half(c), half(b), z[half(a)])
    left_product(2, tab, dbuf, ebuf)
    o = unbutterfly(right_product(2, tab, ebuf))
    g[0] = o[0]
    g[1] = o[1]

    def g_copy(s, c):
        return remote(pool.at[s + 6, c], pool.at[d, c], g_send.at[s, c], g_recv.at[d, c], (s, t))

    def contribute(s):
        slot = jnp.where(s == d, d, s + 6)
        pr, pi = psi[s, 0], psi[s, 1]
        gr, gi = g[0], g[1]
        pool[slot, 0] = pr * gr - pi * gi
        pool[slot, 1] = -(pr * gi + pi * gr)

    def backward(i, _):
        s = 3 - i
        contribute(s)
        through(s, g[0], g[1])
        left_product(0, tab, dbuf, ebuf)
        o = unbutterfly(right_product(0, tab, ebuf))
        g[0] = o[0]
        g[1] = o[1]
        return 0

    lax.fori_loop(0, 3, backward, 0)
    contribute(0)

    def spill_copy(k, c):
        to = jnp.where((odd == 1) & (k >= 2), tile(-1), tile(1))
        return remote(pool.at[k, c], pool.at[k + 10, c], spill_send.at[k, c], spill_recv.at[k, c], (d, to))

    def back_copy(k, c):
        return remote(pool.at[k, c], pool.at[k + 2, c], back_send.at[k - 2, c], back_recv.at[k - 2, c], (d, tile(-2)))

    def send_back(k, c):
        g_copy(k, c).start()

    def pass_on(k):
        for c in both:

            @pl.when(k != d)
            def _():
                remote(pool.at[6, c], pool.at[k, c], g_send.at[0, c], g_recv.at[k, c], (k, t)).wait_recv()

            @pl.when((odd == 1) & (k >= 2))
            def _():
                back_copy(k, c).start()

            spill_copy(k, c).start()

    def mine_of(k, parts=both):
        @pl.when((odd == 1) & (k >= 2))
        def _():
            for c in parts:
                back_copy(k, c).wait_recv()

        return (jnp.where((odd == 1) & (k >= 2), k + 2, k), pos0[0, k], pos0[1, k], True)

    def spilled_of(k, parts=both):
        for c in parts:
            spill_copy(k, c).wait_recv()
        return (k + 10, pos1[0, k], pos1[1, k], False)

    first, second, across = turns[:3]

    @pl.when(odd == 0)
    def _():
        for c in both:
            send_back(first, c)
            send_back(second, c)
        send_back(across, 0)

    @pl.when(odd == 1)
    def _():
        for c in both:
            send_back(first, c)
            send_back(second, c)

    pass_on(d)

    @pl.when(odd == 1)
    def _():
        for c in both:
            g_copy(first, c).wait_send()
            g_copy(second, c).wait_send()
        for c in both:
            send_back(across, c)

    pass_on(first)
    pass_on(second)

    @pl.when(odd == 0)
    def _():
        add_pieces(canvas, pool, [mine_of(d)])
        add_pieces(canvas, pool, [mine_of(first), mine_of(second)])
        pl.semaphore_wait(turn_sem.at[1], 1)
        send_back(across, 1)
        add_pieces(canvas, pool, [spilled_of(d), spilled_of(first), spilled_of(second)])
        pass_on(across)

    @pl.when(odd == 1)
    def _():
        add_pieces(canvas, pool, [mine_of(d)])
        g_copy(across, 0).wait_send()
        pl.semaphore_signal(turn_sem.at[1], inc=1, device_id=(d, t - 1), device_id_type=MESH)
        add_pieces(canvas, pool, [spilled_of(d), spilled_of(first), spilled_of(second)])
        pass_on(across)
        add_pieces(canvas, pool, [mine_of(first), mine_of(second)])

    for c in both:
        add_pieces(canvas, pool, [mine_of(across, (c,)), spilled_of(across, (c,))], (c,))

    info1.wait_send()

    @pl.when(far_slot)
    def _():
        meas_far.wait_send()

    @pl.when(odd == 1)
    def _():
        info2.wait_send()
        for c in both:
            for k in (2, 3):
                far_copy(k, c).wait_send()
                back_copy(k, c).wait_send()
            y_copy(first, c).wait_send()
            y_copy(second, c).wait_send()
        y_copy(across, 0).wait_send()
        g_copy(across, 1).wait_send()

    @pl.when(odd == 0)
    def _():
        for c in both:
            for k in (first, second, across):
                g_copy(k, c).wait_send()

    y_copy(across, 1).wait_send()
    for k in range(4):
        for c in both:
            halo_copy(k, c).wait_send()
            spill_copy(k, c).wait_send()


def solution(mesh):
    depth, tiles = mesh.shape["depth"], mesh.shape["tile"]
    tables, order = transform_tables(), order_table()
    hbm = pl.BlockSpec(memory_space=pl.ANY)
    smem = pl.BlockSpec(memory_space=pltpu.SMEM)
    dma = pltpu.SemaphoreType.DMA

    def pieces(count):
        return pltpu.VMEM((count, *PIECE), F32)

    def local(specimen, positions, occupied, measured, probe_wave):
        columns = specimen.shape[-1]
        canvas = pl.pallas_call(
            functools.partial(gradient_kernel, depth, tiles),
            out_shape=pltpu.VMEM((2, N, columns), F32),
            in_specs=[hbm, smem, smem, hbm, hbm, hbm, hbm],
            out_specs=pl.BlockSpec(memory_space=pltpu.VMEM),
            scratch_shapes=[
                pltpu.VMEM((columns // H, 2, N, H), F32),
                pieces(6), pieces(4), pieces(4), pieces(4), pieces(4), pieces(4),
                pltpu.VMEM(PIECE, F32),
                pltpu.VMEM((2, 2, N, N), BF),
                pltpu.VMEM((2, 2, N, N), BF),
                pieces(14),
                pltpu.VMEM(tables.shape, BF),
                pltpu.VMEM(order.shape, BF),
                pltpu.VMEM((N, N), F32),
                pltpu.VMEM((N, N), F32),
                pltpu.VMEM(PIECE, F32),
                pltpu.SMEM((2, 4), jnp.int32),
                pltpu.SMEM((2, 4), jnp.int32),
                pltpu.SMEM((2, 4), jnp.int32),
                dma((4,)), dma((columns // H,)), dma((2,)), dma((2,)), dma((4, 2)), dma((4, 2)), dma((2, 2)), dma((2, 2)),
                dma((4, 2)), dma((4, 2)), dma((4, 2)), dma((4, 2)), dma((4, 2)), dma((4, 2)), dma((2, 2)), dma((2, 2)),
                dma(()), dma(()), pltpu.SemaphoreType.REGULAR((2,)),
            ],
            compiler_params=pltpu.CompilerParams(
                collective_id=0, has_side_effects=True, vmem_limit_bytes=48 * 2**20
            ),
        )(specimen, positions, occupied, measured, probe_wave, tables, order)
        return canvas[:, None]

    return jax.shard_map(
        local,
        mesh=mesh,
        in_specs=(P(None, "depth", "tile", None), P(None, "tile"), P("tile"), P("tile", None, None), P()),
        out_specs=P(None, "depth", "tile", None),
        check_vma=False,
    )
```

```python
import functools
import math

import jax
import jax.numpy as jnp
import ml_dtypes
import numpy as np
from jax import lax
from jax.experimental import pallas as pl
from jax.experimental.pallas import tpu as pltpu
from jax.sharding import PartitionSpec as P

MESH = pl.DeviceIdType.MESH
BF = jnp.bfloat16
F32 = jnp.float32
N = 256
H = 128
PIECE = (2, N, N)


def transform_tables():
    j = np.arange(N)
    unitary = np.exp(-2j * np.pi * ((j[:, None] * j[None, :]) % N) / N) / math.sqrt(N)
    f = ((j + H) % N) - H
    kernel = np.conj(unitary) @ (np.exp(-12j * f * f / (N * N))[:, None] * unitary)
    kernels = [(kernel[:H, :H] + sign * kernel[:H, H:]) / 2 for sign in (1, -1)]
    halves = [unitary[:H, 0::2], unitary[:H, 1::2]]

    def left(m):
        return np.block([[m.real, -m.imag], [m.imag, m.real]])

    def right(m):
        return np.block([[m.real, m.imag], [-m.imag, m.real]])

    lefts = [[left(m) for m in kernels], [left(m.T) for m in halves], [left(m) for m in halves]]
    rights = [[right(m) for m in kernels], [right(m) for m in halves], [right(m.T) for m in halves]]
    exact = np.array([lefts, rights])
    high = exact.astype(ml_dtypes.bfloat16)
    low = (exact - high.astype(np.float64)).astype(ml_dtypes.bfloat16)
    return np.stack([high, low], axis=3)


def order_table():
    table = np.zeros((N, N))
    table[np.arange(N), np.r_[0:N:2, 1:N:2]] = 1
    return table.astype(ml_dtypes.bfloat16)


def split(x):
    high = x.astype(BF)
    return high, (x - high.astype(F32)).astype(BF)


def dot(a, b):
    return jnp.dot(a, b, preferred_element_type=F32)


def exact_dot(multiply, x):
    high = x.astype(BF)
    rest = x - high.astype(F32)
    middle = rest.astype(BF)
    low = (rest - middle.astype(F32)).astype(BF)
    return multiply(high) + (multiply(middle) + multiply(low))


def put(buf, index, rows, cols, x):
    high, low = split(x)
    buf[index, 0, rows, cols] = high
    buf[index, 1, rows, cols] = low


def half(i):
    return slice(i * H, (i + 1) * H)


def butterfly_store(xr, xi, dbuf):
    for c, x in ((0, xr), (1, xi)):
        top, bottom = x[:H], x[H:]
        for a, y in ((0, top + bottom), (1, top - bottom)):
            put(dbuf, a, half(c), half(0), y[:, :H] + y[:, H:])
            put(dbuf, a, half(c), half(1), y[:, :H] - y[:, H:])


def left_product(kind, tab, dbuf, ebuf):
    for a in range(2):
        high, low = dbuf[a, 0], dbuf[a, 1]
        e = dot(tab[0, kind, a, 0], high) + (dot(tab[0, kind, a, 0], low) + dot(tab[0, kind, a, 1], high))
        for c in range(2):
            for b in range(2):
                put(ebuf, b, half(a), half(c), e[half(c), half(b)])


def right_product(kind, tab, ebuf):
    out = []
    for b in range(2):
        high, low = ebuf[b, 0], ebuf[b, 1]
        out.append(dot(high, tab[1, kind, b, 0]) + (dot(low, tab[1, kind, b, 0]) + dot(high, tab[1, kind, b, 1])))
    return out


def unbutterfly(g):
    res = []
    for c in range(2):
        p, m = g[0][:, half(c)], g[1][:, half(c)]
        y = jnp.concatenate([p + m, p - m], axis=1)
        res.append(jnp.concatenate([y[:H] + y[H:], y[:H] - y[H:]], axis=0))
    return res


def cut(spec, row, col, top, store):
    block = lax.div(col, H)
    rem = lax.rem(col, H)
    odd = lax.rem(block, 2)
    chunk = 32

    def body(i, _):
        rows = pl.ds(pl.multiple_of(i * chunk, chunk), chunk)
        lane = lax.broadcasted_iota(jnp.int32, (chunk, H), 1)
        line = lax.broadcasted_iota(jnp.int32, (chunk, H), 0) + i * chunk
        keep = line >= row if top else line < row
        for side in range(2):
            first = block + (odd if side == 0 else 1 - odd)
            second = first + 2 - 2 * lax.div(first + 2, 32)
            limit = rem * (1 - odd if side == 0 else odd)
            for c in range(2):
                here = spec[first, c, rows, :]
                there = spec[second, c, rows, :]
                store(c, rows, half(side), jnp.where(keep, jnp.where(lane >= limit, here, there), 0.0))
        return 0

    lax.fori_loop(0, N // chunk, body, 0)


def add_pieces(canvas, pool, pieces, parts=range(4)):
    chunk = 16

    def body(i, _):
        rows = pl.ds(pl.multiple_of(i * chunk, chunk), chunk)
        lane = lax.broadcasted_iota(jnp.int32, (chunk, H), 1)
        for part in parts:
            c, first = part // 2, part % 2 * H
            line = lax.broadcasted_iota(jnp.int32, (chunk, H), 0) + (first + i * chunk)
            here = pl.ds(pl.multiple_of(first + i * chunk, chunk), chunk)
            values = [
                [jnp.where(line >= row if top else line < row, pool[slot, part, rows, half(h)], 0.0) for h in range(2)]
                for slot, row, _, top in pieces
            ]
            for b in range(canvas.shape[2] // H):
                total = canvas[c, here, half(b)]
                for value, (_, _, col, _) in zip(values, pieces):
                    at = lane + (b * H - col)
                    total += jnp.where((at >= 0) & (at < N), value[b % 2], 0.0)
                canvas[c, here, half(b)] = total
        return 0

    lax.fori_loop(0, H // chunk, body, 0)


def gradient_kernel(
    depth, tiles, specimen, positions, occupied, measured, probe, tables, order, canvas,
    spec, mine, halo_out, halo_in, merged, waves, psi, g, dbuf, ebuf, pool, tab, perm, meas, mp,
    wave0, pos0, pos1, pos2,
    load_sem, spec_sem, info_send, info_recv, halo_send, halo_recv, far_send, far_recv, y_send, y_recv,
    g_send, g_recv, spill_send, spill_recv, back_send, back_recv, meas_send, meas_recv, turn_sem,
):
    d = lax.axis_index("depth")
    t = lax.axis_index("tile")
    odd = lax.rem(t, 2)
    both = range(2)
    parts = range(4)

    def tile(k):
        return lax.rem(t + k + tiles, tiles)

    def level(k):
        return lax.rem(d + k, depth)

    def remote(src, dst, send, recv, to):
        return pltpu.make_async_remote_copy(
            src_ref=src, dst_ref=dst, send_sem=send, recv_sem=recv, device_id=to, device_id_type=MESH
        )

    near = lax.rem(d + 1, 2)
    turns = (near, near + 2, level(2), d)
    far_slot = (odd == 1) & (d >= 2)

    probe_load = pltpu.make_async_copy(probe, wave0, load_sem.at[0])
    order_load = pltpu.make_async_copy(order, perm, load_sem.at[1])
    tables_load = pltpu.make_async_copy(tables, tab, load_sem.at[2])
    meas_load = pltpu.make_async_copy(measured.at[d], meas, load_sem.at[3])
    blocks = spec.shape[0]

    def block_load(b):
        cols = pl.ds(pl.multiple_of(b * H, H), H)
        return pltpu.make_async_copy(specimen.at[:, 0, :, cols], spec.at[b], spec_sem.at[b])

    lax.fori_loop(0, blocks, lambda b, _: (block_load(b).start(), 0)[1], 0)
    barrier = pltpu.get_barrier_semaphore()
    partners = [(level(k), t) for k in range(1, 4)] + [(d, tile(k)) for k in (-1, 1)]
    wide = [(d, tile(k)) for k in (-2, 2)]
    for partner in partners:
        pl.semaphore_signal(barrier, inc=1, device_id=partner, device_id_type=MESH)

    @pl.when(odd == 1)
    def _():
        for partner in wide:
            pl.semaphore_signal(barrier, inc=1, device_id=partner, device_id_type=MESH)

    for k in range(4):
        pos0[0, k] = (positions[0, k] - t * N) * occupied[k]
        pos0[1, k] = positions[1, k]

    def cut_top(k):
        def store(c, rows, cols, x):
            mine[k, c, rows, cols] = x

        cut(spec, pos0[0, k] + N * (1 - occupied[k]), pos0[1, k], True, store)

    def turn_probe(row, col):
        line = lax.broadcasted_iota(jnp.int32, (N, N), 0)
        lane = lax.broadcasted_iota(jnp.int32, (N, N), 1)
        turn_rows = (lax.bitwise_and(line - lane - row, N - 1) == 0).astype(F32).astype(BF)
        turn_cols = (lax.bitwise_and(lane - line - col, N - 1) == 0).astype(F32).astype(BF)
        for c in both:
            turned = exact_dot(lambda x: dot(turn_rows, x), wave0[c])
            psi[0, c] = exact_dot(lambda x: dot(x, turn_cols), turned)

    def order_measured():
        high, low = split(meas[...])
        high, low = split(dot(perm[...], high) + dot(perm[...], low))
        across = (((1,), (1,)), ((), ()))
        mp[...] = lax.dot_general(high, perm[...], across, preferred_element_type=F32) + lax.dot_general(
            low, perm[...], across, preferred_element_type=F32
        )

    def clear(i, _):
        rows = pl.ds(pl.multiple_of(i * 8, 8), 8)
        for c in both:
            canvas[c, rows, :] = jnp.zeros((8, canvas.shape[2]), F32)
        return 0

    pl.semaphore_wait(barrier, jnp.where(odd == 1, len(partners) + len(wide), len(partners)))

    info1 = remote(pos0, pos1, info_send.at[0], info_recv.at[0], (d, tile(1)))
    info2 = remote(pos0, pos2, info_send.at[1], info_recv.at[1], (d, tile(2)))
    meas_far = remote(measured.at[d], meas, meas_send, meas_recv, (d, tile(2)))

    def far_copy(k, c):
        return remote(mine.at[k, c], mine.at[k + 2, c], far_send.at[k - 2, c], far_recv.at[k - 2, c], (d, tile(2)))

    def halo_copy(k, c):
        to = jnp.where((odd == 1) | (k < 2), tile(-1), tile(1))
        return remote(halo_out.at[k, c], halo_in.at[k, c], halo_send.at[k, c], halo_recv.at[k, c], (d, to))

    info1.start()

    @pl.when(odd == 1)
    def _():
        info2.start()

    lax.fori_loop(0, blocks, lambda b, _: (block_load(b).wait(), 0)[1], 0)
    probe_load.start()
    order_load.start()

    @pl.when(jnp.logical_not(far_slot))
    def _():
        meas_load.start()

    tables_load.start()

    info1.wait_recv()

    def cut_bottom(k):
        def store(c, rows, cols, x):
            halo_out[k, c, rows, cols] = x

        cut(spec, pos1[0, k], pos1[1, k], False, store)
        for c in both:
            halo_copy(k, c).start()

    def cut_mine(k):
        @pl.when((odd == 0) | (k < 2))
        def _():
            cut_top(k)

    cut_bottom(turns[0])
    cut_bottom(turns[1])

    @pl.when(odd == 1)
    def _():
        for k in (near + 2, 3 - near):
            cut_top(k)
            for c in both:
                far_copy(k, c).start()

    @pl.when(far_slot)
    def _():
        meas_far.start()

    cut_bottom(turns[2])
    cut_bottom(turns[3])
    cut_mine(turns[0])
    cut_mine(turns[1])

    def y_copy(k, c):
        return remote(merged.at[k, c], waves.at[d, c], y_send.at[k, c], y_recv.at[d, c], (k, t))

    def merge(k, c, dst):
        halo_copy(k, c).wait_recv()

        @pl.when((odd == 1) & (k >= 2))
        def _():
            far_copy(k, c).wait_recv()

        source = jnp.where((odd == 1) & (k >= 2), k + 2, k)

        def body(i, _):
            rows = pl.ds(pl.multiple_of(i * 64, 64), 64)
            dst[c, rows, :] = mine[source, c, rows, :] + halo_in[k, c, rows, :]
            return 0

        lax.fori_loop(0, N // 64, body, 0)

    def merge_level(k):
        for c in both:
            merge(k, c, merged.at[k])

    def send_level(k):
        for c in both:
            y_copy(k, c).start()

    merge_level(turns[0])
    merge_level(turns[1])

    @pl.when(odd == 0)
    def _():
        send_level(turns[0])
        send_level(turns[1])
        cut_mine(turns[2])
        merge_level(turns[2])
        send_level(turns[2])
        cut_mine(turns[3])

    @pl.when(odd == 1)
    def _():
        cut_mine(turns[2])
        cut_mine(turns[3])

    @pl.when(odd == 1)
    def _():
        info2.wait_recv()

    probe_load.wait()
    turn_probe(jnp.where(far_slot, pos2[0, d], pos0[0, d]), jnp.where(far_slot, pos2[1, d], pos0[1, d]))
    lax.fori_loop(0, N // 8, clear, 0)

    @pl.when(odd == 1)
    def _():
        pl.semaphore_wait(turn_sem.at[0], 1)
        send_level(turns[0])
        send_level(turns[1])
        merge_level(turns[2])
        send_level(turns[2])

    for c in both:
        merge(d, c, waves.at[d])

    @pl.when(odd == 0)
    def _():
        for k in turns[:2]:
            for c in both:
                y_copy(k, c).wait_send()
        y_copy(turns[2], 0).wait_send()
        pl.semaphore_signal(turn_sem.at[0], inc=1, device_id=(d, t + 1), device_id_type=MESH)

    order_load.wait()

    @pl.when(far_slot)
    def _():
        meas_far.wait_recv()

    @pl.when(jnp.logical_not(far_slot))
    def _():
        meas_load.wait()

    order_measured()
    tables_load.wait()

    def arrived(s):
        @pl.when(s != d)
        def _():
            for c in both:
                remote(merged.at[0, c], waves.at[s, c], y_send.at[0, c], y_recv.at[s, c], (s, t)).wait_recv()

    def through(s, vr, vi):
        tr, ti = waves[s, 0], waves[s, 1]
        butterfly_store(tr * vr - ti * vi, tr * vi + ti * vr, dbuf)

    def forward(s, _):
        arrived(s)
        through(s, psi[s, 0], psi[s, 1])
        left_product(0, tab, dbuf, ebuf)
        o = unbutterfly(right_product(0, tab, ebuf))
        psi[s + 1, 0] = o[0]
        psi[s + 1, 1] = o[1]
        return 0

    lax.fori_loop(0, 3, forward, 0)
    arrived(3)

    through(3, psi[3, 0], psi[3, 1])
    left_product(1, tab, dbuf, ebuf)
    far = right_product(1, tab, ebuf)
    for b in both:
        fr, fi = far[b][:, :H], far[b][:, H:]
        excess = fr * fr + fi * fi - mp[:, half(b)]
        for c, z in ((0, excess * fr), (1, -(excess * fi))):
            for a in both:
                put(dbuf, a, half(c), half(b), z[half(a)])
    left_product(2, tab, dbuf, ebuf)
    o = unbutterfly(right_product(2, tab, ebuf))
    g[0] = o[0]
    g[1] = o[1]

    def g_copy(s, c):
        return remote(pool.at[s + 6, c], pool.at[d, c], g_send.at[s, c], g_recv.at[d, c], (s, t))

    def contribute(s):
        slot = jnp.where(s == d, d, s + 6)
        pr, pi = psi[s, 0], psi[s, 1]
        gr, gi = g[0], g[1]
        for c, x in ((0, pr * gr - pi * gi), (1, -(pr * gi + pi * gr))):
            pool[slot, 2 * c] = x[:H]
            pool[slot, 2 * c + 1] = x[H:]

    def backward(i, _):
        s = 3 - i
        contribute(s)
        through(s, g[0], g[1])
        left_product(0, tab, dbuf, ebuf)
        o = unbutterfly(right_product(0, tab, ebuf))
        g[0] = o[0]
        g[1] = o[1]
        return 0

    lax.fori_loop(0, 3, backward, 0)
    contribute(0)

    def spill_copy(k, c):
        to = jnp.where((odd == 1) & (k >= 2), tile(-1), tile(1))
        return remote(pool.at[k, c], pool.at[k + 10, c], spill_send.at[k, c], spill_recv.at[k, c], (d, to))

    def back_copy(k, c):
        return remote(pool.at[k, c], pool.at[k + 2, c], back_send.at[k - 2, c], back_recv.at[k - 2, c], (d, tile(-2)))

    def send_back(k, c):
        g_copy(k, c).start()

    def pass_on(k):
        for c in parts:

            @pl.when(k != d)
            def _():
                remote(pool.at[6, c], pool.at[k, c], g_send.at[0, c], g_recv.at[k, c], (k, t)).wait_recv()

            @pl.when((odd == 1) & (k >= 2))
            def _():
                back_copy(k, c).start()

            spill_copy(k, c).start()

    def mine_of(k, parts=range(4)):
        @pl.when((odd == 1) & (k >= 2))
        def _():
            for c in parts:
                back_copy(k, c).wait_recv()

        return (jnp.where((odd == 1) & (k >= 2), k + 2, k), pos0[0, k], pos0[1, k], True)

    def spilled_of(k, parts=range(4)):
        for c in parts:
            spill_copy(k, c).wait_recv()
        return (k + 10, pos1[0, k], pos1[1, k], False)

    first, second, across = turns[:3]

    @pl.when(odd == 0)
    def _():
        for c in parts:
            send_back(first, c)
            send_back(second, c)
        send_back(across, 0)
        send_back(across, 1)

    @pl.when(odd == 1)
    def _():
        for c in parts:
            send_back(first, c)
            send_back(second, c)

    pass_on(d)

    @pl.when(odd == 1)
    def _():
        for c in parts:
            g_copy(first, c).wait_send()
            g_copy(second, c).wait_send()
        for c in parts:
            send_back(across, c)

    pass_on(first)
    pass_on(second)

    @pl.when(odd == 0)
    def _():
        add_pieces(canvas, pool, [mine_of(d)])
        add_pieces(canvas, pool, [mine_of(first), mine_of(second)])
        pl.semaphore_wait(turn_sem.at[1], 1)
        send_back(across, 2)
        send_back(across, 3)
        add_pieces(canvas, pool, [spilled_of(d), spilled_of(first), spilled_of(second)])
        pass_on(across)

    @pl.when(odd == 1)
    def _():
        add_pieces(canvas, pool, [mine_of(d)])
        g_copy(across, 0).wait_send()
        g_copy(across, 1).wait_send()
        pl.semaphore_signal(turn_sem.at[1], inc=1, device_id=(d, t - 1), device_id_type=MESH)
        add_pieces(canvas, pool, [spilled_of(d), spilled_of(first), spilled_of(second)])
        pass_on(across)
        add_pieces(canvas, pool, [mine_of(first), mine_of(second)])

    for part in parts:
        add_pieces(canvas, pool, [mine_of(across, (part,)), spilled_of(across, (part,))], (part,))

    info1.wait_send()

    @pl.when(far_slot)
    def _():
        meas_far.wait_send()

    @pl.when(odd == 1)
    def _():
        info2.wait_send()
        for c in both:
            for k in (2, 3):
                far_copy(k, c).wait_send()
            y_copy(first, c).wait_send()
            y_copy(second, c).wait_send()
        y_copy(across, 0).wait_send()
        for part in parts:
            back_copy(2, part).wait_send()
            back_copy(3, part).wait_send()
        g_copy(across, 2).wait_send()
        g_copy(across, 3).wait_send()

    @pl.when(odd == 0)
    def _():
        for part in parts:
            for k in (first, second, across):
                g_copy(k, part).wait_send()

    y_copy(across, 1).wait_send()
    for k in range(4):
        for c in both:
            halo_copy(k, c).wait_send()
        for part in parts:
            spill_copy(k, part).wait_send()


def solution(mesh):
    depth, tiles = mesh.shape["depth"], mesh.shape["tile"]
    tables, order = transform_tables(), order_table()
    hbm = pl.BlockSpec(memory_space=pl.ANY)
    smem = pl.BlockSpec(memory_space=pltpu.SMEM)
    dma = pltpu.SemaphoreType.DMA

    def pieces(count):
        return pltpu.VMEM((count, *PIECE), F32)

    def local(specimen, positions, occupied, measured, probe_wave):
        columns = specimen.shape[-1]
        canvas = pl.pallas_call(
            functools.partial(gradient_kernel, depth, tiles),
            out_shape=pltpu.VMEM((2, N, columns), F32),
            in_specs=[hbm, smem, smem, hbm, hbm, hbm, hbm],
            out_specs=pl.BlockSpec(memory_space=pltpu.VMEM),
            scratch_shapes=[
                pltpu.VMEM((columns // H, 2, N, H), F32),
                pieces(6), pieces(4), pieces(4), pieces(4), pieces(4), pieces(4),
                pltpu.VMEM(PIECE, F32),
                pltpu.VMEM((2, 2, N, N), BF),
                pltpu.VMEM((2, 2, N, N), BF),
                pltpu.VMEM((14, 4, H, N), F32),
                pltpu.VMEM(tables.shape, BF),
                pltpu.VMEM(order.shape, BF),
                pltpu.VMEM((N, N), F32),
                pltpu.VMEM((N, N), F32),
                pltpu.VMEM(PIECE, F32),
                pltpu.SMEM((2, 4), jnp.int32),
                pltpu.SMEM((2, 4), jnp.int32),
                pltpu.SMEM((2, 4), jnp.int32),
                dma((4,)), dma((columns // H,)), dma((2,)), dma((2,)), dma((4, 2)), dma((4, 2)), dma((2, 2)), dma((2, 2)),
                dma((4, 2)), dma((4, 2)), dma((4, 4)), dma((4, 4)), dma((4, 4)), dma((4, 4)), dma((2, 4)), dma((2, 4)),
                dma(()), dma(()), pltpu.SemaphoreType.REGULAR((2,)),
            ],
            compiler_params=pltpu.CompilerParams(
                collective_id=0, has_side_effects=True, vmem_limit_bytes=48 * 2**20
            ),
        )(specimen, positions, occupied, measured, probe_wave, tables, order)
        return canvas[:, None]

    return jax.shard_map(
        local,
        mesh=mesh,
        in_specs=(P(None, "depth", "tile", None), P(None, "tile"), P("tile"), P("tile", None, None), P()),
        out_specs=P(None, "depth", "tile", None),
        check_vma=False,
    )
```
